32 devices in a mesh: group: 2 (over x), replica: 8 (over z, y), tensor: 2 (over core).
Axes of the slice: x: 2, y: 2, z: 4, core: 2. Of those that a mesh axis runs over, the one named last changes fastest.
Arguments:
- cache: bfloat16 [16, 8, 384, 8, 256], P(('group', 'replica'), None, None, 'tensor'), parts along dimension 0, may hold values from -6 to 6
- lengths: int32 [16, 8], P('group'), parts along dimension 0, may hold values from 2 to 383, as said below
- partner: int32 [16], P('group'), parts along dimension 0, may hold values from 0 to 7, as said below
- migrant: int32 [16, 2], P('group'), parts along dimension 0, may hold values from 0 to 7, as said below
- replica_prefill_pages: bfloat16 [16, 4, 16, 8, 256], P(('group', 'replica'), None, None, 'tensor'), parts along dimension 0, may hold values from -6 to 6
- page_dest: int32 [16, 4, 1], P('group'), parts along dimension 0, may hold values from 0 to 7; in each aligned block of 4 rows (0 to 3, 4 to 7, ..., all dimensions but the last counted through in order) at most 2 rows name the same one
- landing: int32 [16, 192], P(('group', 'replica')), parts along dimension 0, may hold values from 0 to 191, each once within a row
- query: bfloat16 [16, 8, 64, 128], P(('group', 'replica'), None, 'tensor'), parts along dimension 0, may hold values from -128 to 128
- fresh_key_value: bfloat16 [16, 8, 8, 256], P(('group', 'replica'), None, 'tensor'), parts along dimension 0, may hold values from -6 to 6
Outputs:
- cache_out: bfloat16 [16, 8, 384, 8, 256], P(('group', 'replica'), None, None, 'tensor'), parts along dimension 0
- attended: bfloat16 [16, 8, 64, 128], P(('group', 'replica'), None, 'tensor'), parts along dimension 0
The draws below stay inside these ranges and needn't reach their ends.
There are 2 independent parts, one for each index of `group`. The reference program is written for one: setup_inputs(seed, part) draws one part's arguments, and reference() takes and returns one part's arrays. A program takes and returns all parts, laid end to end along the dimension named above; each array names one. Nothing has to cross between parts.
Inputs may be any that keep to these rules, and one draw needn't show every extreme that they name: `lengths`: in every replica some request has 383 cached tokens. partner[r] differs from r in exactly one bit of its index, and partner[partner[r]] = r. `migrant`: the two slots of a replica differ. `page_dest`: of the pages of one replica, at most 2 go to the same destination. `landing`: each row is a permutation of the 192 pages.
All inputs are finite; a program needn't handle non-finite values.
Results may differ from the reference program's by a relative error of at most 0.005.
Values may be sent and summed in bfloat16 or wider, within the bound.
A program may use at most 128 MiB of HBM per device.

```python
import math
import jax
import jax.numpy as jnp
import numpy as np
from jax import lax

QUERY_HEADS = 64
KEY_VALUE_HEADS = 8
HEAD_SIZE = 128
REQUEST_SLOTS = 8
PAGE_TOKENS = 16
PAGES_REQ = 24
CAP = 2
SLOT_LENGTH = 384
REPLICA_COUNT = 8
PREFILL_PAGES = 4


def shared_rows(key):
    key = jax.random.fold_in(key, 100)
    key_matrix = jax.random.fold_in(key, 0)
    leading_part = jax.random.truncated_normal(key_matrix, -6.0, 6.0, (REPLICA_COUNT, REQUEST_SLOTS, 2, KEY_VALUE_HEADS, 2 * HEAD_SIZE), jnp.float32)
    return leading_part


def draw_cache(key, part):
    leading_part = shared_rows(key)
    key = jax.random.fold_in(key, 3)
    remaining_part = jax.random.truncated_normal(key, -6.0, 6.0, (REPLICA_COUNT, REQUEST_SLOTS, SLOT_LENGTH - 2, KEY_VALUE_HEADS, 2 * HEAD_SIZE), jnp.float32)
    return jnp.concatenate([leading_part, remaining_part], axis=2).astype(jnp.bfloat16)


def draw_query(key, part):
    key = jax.random.fold_in(key, 5)
    normal_rows = jax.random.truncated_normal(key, -6.0, 6.0, (REPLICA_COUNT, REQUEST_SLOTS, QUERY_HEADS, HEAD_SIZE), jnp.float32)
    return normal_rows.astype(jnp.bfloat16)


def draw_lengths(key, part):
    key = jax.random.fold_in(key, 7)
    key_len, key_selection = jax.random.split(key, 2)
    drawn = jax.random.randint(key_len, (REPLICA_COUNT, REQUEST_SLOTS), 2, SLOT_LENGTH)
    longest = jax.random.randint(key_selection, (REPLICA_COUNT, 1), 0, REQUEST_SLOTS)
    return jnp.where(jnp.arange(REQUEST_SLOTS)[None, :] == longest, SLOT_LENGTH - 1, drawn).astype(jnp.int32)


def draw_partner(key, part):
    key = jax.random.fold_in(key, 11)
    bit_count = REPLICA_COUNT.bit_length() - 1
    key_split, key_low, key_high = jax.random.split(key, 3)
    split_bit = jax.random.randint(key_split, (), 0, bit_count)
    low_bit = jax.random.randint(key_low, (), 0, bit_count - 1)
    low_bit = low_bit + (low_bit >= split_bit).astype(jnp.int32)
    high_bit = jax.random.randint(key_high, (), 0, bit_count - 1)
    high_bit = high_bit + (high_bit >= split_bit).astype(jnp.int32)
    nodes = jnp.arange(REPLICA_COUNT, dtype=jnp.int32)
    side_bit = jnp.bitwise_and(jnp.right_shift(nodes, split_bit), 1)
    chosen_bit = jnp.where(side_bit == 0, low_bit, high_bit)
    return jnp.bitwise_xor(nodes, jnp.left_shift(jnp.int32(1), chosen_bit)).astype(jnp.int32)


def draw_migrant(key, part):
    key = jax.random.fold_in(key, 13)
    key_first, key_offset = jax.random.split(key, 2)
    first_slot = jax.random.randint(key_first, (REPLICA_COUNT,), 0, REQUEST_SLOTS)
    offset = jax.random.randint(key_offset, (REPLICA_COUNT,), 1, REQUEST_SLOTS)
    second_slot = (first_slot + offset) % REQUEST_SLOTS
    return jnp.stack([first_slot, second_slot], axis=1).astype(jnp.int32)


def level_of(stream_key, extent, cuts, least, largest):
    loudness = 1.0
    for position, blocks in cuts:
        heights = jax.random.uniform(jax.random.fold_in(jax.random.fold_in(stream_key, 6), position), (blocks,), jnp.float32, least / len(cuts), largest / len(cuts))
        loudness = loudness * jnp.repeat(jnp.exp(heights), extent[position] // blocks).reshape((-1,) + (1,) * (len(extent) - 1 - position))
    return loudness


def routed_block(stream_key, own, number, rows, amount, top, reach, skew):
    order = jax.random.permutation(stream_key, amount)
    heavy_load, common = portions_of(amount, rows * top, reach, skew, True), portions_of(amount, rows * top, reach, skew, False)
    places = jnp.arange(amount)

    def named(sizes, rotation):
        used = int((sizes > 0).sum())
        fixed = max(1, used // 4)
        shifted = fixed + (places - fixed + rotation * (used - fixed)) % max(1, amount - fixed)
        return jnp.zeros((amount,), jnp.int32).at[order[jnp.where(places < fixed, places, shifted)]].set(jnp.asarray(sizes, jnp.int32))

    sizes = jnp.where(number % 4 == 0, named(heavy_load, number // 4), named(common, number - number // 4 - 1))
    mixed = jax.random.permutation(jax.random.fold_in(own, 3), amount)
    giver, taker = mixed[0:amount // 2 * 2:2], mixed[1:amount // 2 * 2:2]
    room = jnp.minimum(sizes[giver] - 1, reach - sizes[taker]) // 2
    room = jnp.where((giver == order[0]) | (taker == order[0]) | (sizes[taker] == 0), 0, jnp.maximum(room, 0))
    shifted = jax.random.randint(jax.random.fold_in(own, 4), (amount // 2,), 0, 1 << 20) % (room + 1)
    sizes = sizes.at[giver].add(-shifted).at[taker].add(shifted)
    items = jnp.searchsorted(jnp.cumsum(sizes), jnp.arange(rows * top), side="right").astype(jnp.int32)
    listing = items.reshape(top, rows).T
    listing = listing[jax.random.permutation(jax.random.fold_in(own, 1), rows)]
    rotation = jax.random.randint(jax.random.fold_in(own, 2), (rows, 1), 0, top)
    return jnp.take_along_axis(listing, (jnp.arange(top)[None, :] + rotation) % top, axis=1)


def portions_of(amount, total, reach, lean, full):
    portions = [(1 << 20) // math.isqrt(standing ** lean) + 1 for standing in range(1, amount + 1)]
    largest = reach if full else min(reach, max(-(-total // amount), total * portions[0] // sum(portions)))
    least = 1 if total - largest >= amount - 1 else 0
    counts, surplus = [largest] + [least] * (amount - 1), total - largest - least * (amount - 1)
    while surplus > 0:
        free = [i for i in range(1, amount) if counts[i] < largest] or [i for i in range(1, amount) if counts[i] < reach]
        whole, budget = sum([portions[i] for i in free]), surplus
        for i in free:
            extra = min(reach - counts[i], max(1, budget * portions[i] // whole), surplus)
            counts[i] = counts[i] + extra
            surplus = surplus - extra
    return np.array(counts)


def normal_values(stream_key, shape, deviation, most, cuts=(), kind=jnp.bfloat16):
    factor_of = level_of(stream_key, shape, cuts, -0.22, 0.18) if cuts else 1.0
    entries = jax.random.normal(stream_key, shape, jnp.float32) * deviation * factor_of
    return jnp.minimum(jnp.maximum(entries, -most), most).astype(kind)


def setup_inputs(seed: int = 0, part: int = 0) -> dict:
    keys = jax.random.split(jax.random.key(seed), 10)
    own_keys = jax.random.split(jax.random.fold_in(keys[9], part), 10)
    cache = draw_cache(jax.random.fold_in(jax.random.fold_in(keys[9], part), 71), part)
    lengths = draw_lengths(jax.random.fold_in(jax.random.fold_in(keys[9], part), 71), part)
    partner = draw_partner(jax.random.fold_in(jax.random.fold_in(keys[9], part), 71), part)
    migrant = draw_migrant(jax.random.fold_in(jax.random.fold_in(keys[9], part), 71), part)
    replica_prefill_pages = normal_values(own_keys[4], (REPLICA_COUNT, PREFILL_PAGES, PAGE_TOKENS, KEY_VALUE_HEADS, 2 * HEAD_SIZE), 1.0, 6.0, ((0, 8), (3, 2)))
    page_dest_keys = jax.random.split(jax.random.fold_in(own_keys[5], 1), REPLICA_COUNT * PREFILL_PAGES // PREFILL_PAGES)
    page_dest_turns = jax.random.permutation(jax.random.fold_in(own_keys[5], 3), REPLICA_COUNT * PREFILL_PAGES // PREFILL_PAGES)
    page_dest = jax.vmap(lambda own, number: routed_block(jax.random.fold_in(own_keys[5], 2), own, number, PREFILL_PAGES, REPLICA_COUNT, 1, CAP, 2))(page_dest_keys, page_dest_turns).reshape((REPLICA_COUNT, PREFILL_PAGES, 1))
    landing = jax.vmap(lambda own: jax.random.permutation(own, REQUEST_SLOTS * PAGES_REQ))(jax.random.split(own_keys[6], REPLICA_COUNT)).reshape((REPLICA_COUNT, REQUEST_SLOTS * PAGES_REQ)).astype(jnp.int32)
    query = draw_query(jax.random.fold_in(jax.random.fold_in(keys[9], part), 71), part)
    fresh_key_value = normal_values(own_keys[8], (REPLICA_COUNT, REQUEST_SLOTS, KEY_VALUE_HEADS, 2 * HEAD_SIZE), 1.0, 6.0, ((0, 8), (2, 2)))
    return {"cache": cache, "lengths": lengths, "partner": partner, "migrant": migrant, "replica_prefill_pages": replica_prefill_pages, "page_dest": page_dest, "landing": landing, "query": query, "fresh_key_value": fresh_key_value}


def attend_one(cache_rows, query_matrix, visible_len):
    key_matrix = cache_rows[..., :HEAD_SIZE].astype(jnp.float32)
    value_rows = cache_rows[..., HEAD_SIZE:].astype(jnp.float32)
    grouped_heads = query_matrix.astype(jnp.float32).reshape(REQUEST_SLOTS, KEY_VALUE_HEADS, QUERY_HEADS // KEY_VALUE_HEADS, HEAD_SIZE)
    scores = jnp.einsum('rkgd,rlkd->rkgl', grouped_heads, key_matrix) / math.sqrt(HEAD_SIZE)
    visible = jnp.arange(SLOT_LENGTH)[None, :] <= visible_len[:, None]
    scores = jnp.where(visible[:, None, None, :], scores, -1e+30)
    row_max = lax.optimization_barrier(jnp.max(scores, axis=-1, keepdims=True))
    weights = jnp.exp(scores - row_max)
    soft_weights = (weights / lax.optimization_barrier(jnp.sum(weights, axis=-1, keepdims=True))).astype(jnp.bfloat16)
    soft_weights = lax.optimization_barrier(soft_weights).astype(jnp.float32)
    combined = jnp.einsum('rkgl,rlkd->rkgd', soft_weights, value_rows)
    return combined.reshape(REQUEST_SLOTS, QUERY_HEADS, HEAD_SIZE).astype(jnp.bfloat16)

def reference(cache, lengths, partner, migrant, replica_prefill_pages, page_dest, landing, query, fresh_key_value):
    replica_ids = jnp.arange(REPLICA_COUNT)
    source_slot = migrant[partner]
    moved = cache[partner[:, None], source_slot]
    migrated_state = cache.at[replica_ids[:, None], migrant].set(moved)
    lengths_post = lengths.at[replica_ids[:, None], migrant].set(lengths[partner[:, None], source_slot])
    destinations = page_dest[:, :, 0].reshape(-1)
    hits = (destinations[:, None] == replica_ids[None, :]).astype(jnp.int32)
    arrival_rank = lax.optimization_barrier(jnp.sum(jnp.cumsum(hits, axis=0) * hits, axis=1)) - 1
    landed = landing[destinations, arrival_rank]
    pooled_pages = REQUEST_SLOTS * PAGES_REQ
    flattened_index = destinations * pooled_pages + landed
    page_layout = migrated_state.reshape(REPLICA_COUNT * pooled_pages, PAGE_TOKENS, KEY_VALUE_HEADS, 2 * HEAD_SIZE)
    page_layout = page_layout.at[flattened_index].set(replica_prefill_pages.reshape(REPLICA_COUNT * PREFILL_PAGES, PAGE_TOKENS, KEY_VALUE_HEADS, 2 * HEAD_SIZE))
    delivered_pages = page_layout.reshape(REPLICA_COUNT, REQUEST_SLOTS, SLOT_LENGTH, KEY_VALUE_HEADS, 2 * HEAD_SIZE)
    cache_out = delivered_pages.at[replica_ids[:, None], jnp.arange(REQUEST_SLOTS)[None, :], lengths_post].set(fresh_key_value)
    attended = lax.map(lambda items: attend_one(items[0], items[1], items[2]), (cache_out, query, lengths_post))
    return (cache_out, attended)
```

```python
import functools
import math

import jax
import jax.numpy as jnp
from jax import lax
from jax.experimental import pallas as pl
from jax.experimental.pallas import tpu as pltpu
from jax.sharding import PartitionSpec as P

CAP = 2


def pick_kernel(migrant_ref, cache_ref, out_ref, sems):
    me = lax.axis_index("replica")
    copies = [
        pltpu.make_async_copy(cache_ref.at[0, migrant_ref[me, m]], out_ref.at[m], sems.at[m])
        for m in range(2)
    ]
    for copy in copies:
        copy.start()
    for copy in copies:
        copy.wait()


def finish_kernel(
    lengths_ref,
    partner_ref,
    migrant_ref,
    dest_ref,
    landing_ref,
    cache_ref,
    arrived_ref,
    pages_ref,
    query_ref,
    fresh_ref,
    out_ref,
    attended_ref,
    held,
    load_sems,
    page_sems,
    store_sems,
):
    me = lax.axis_index("replica")
    slots, span, kv_heads, width = held.shape
    head_dim = width // 2
    heads = query_ref.shape[2]
    per_kv = heads // kv_heads
    page_len = pages_ref.shape[1]
    per_slot = span // page_len
    first, second = migrant_ref[me, 0], migrant_ref[me, 1]
    other = partner_ref[me]

    def load(slot, source):
        return pltpu.make_async_copy(source, held.at[slot], load_sems.at[slot])

    for slot in range(slots):
        staying = jnp.logical_and(first != slot, second != slot)

        @pl.when(staying)
        def _():
            load(slot, cache_ref.at[0, slot]).start()

    load(first, arrived_ref.at[0]).start()
    load(second, arrived_ref.at[1]).start()
    for slot in range(slots):
        load(slot, cache_ref.at[0, slot]).wait()

    def page_copy(page, rank):
        place = landing_ref[0, rank]
        slot = place // per_slot
        start = (place - slot * per_slot) * page_len
        return pltpu.make_async_copy(
            pages_ref.at[page], held.at[slot, pl.ds(start, page_len)], page_sems.at[rank]
        )

    def send_page(page, rank):
        mine = dest_ref[page] == me

        @pl.when(mine)
        def _():
            page_copy(page, rank).start()

        return rank + mine.astype(jnp.int32)

    arrivals = lax.fori_loop(0, dest_ref.shape[0], send_page, jnp.int32(0))

    def wait_page(rank, carry):
        page_copy(0, rank).wait()
        return carry

    lax.fori_loop(0, arrivals, wait_page, 0)

    shape = (heads, span * kv_heads)
    columns = lax.broadcasted_iota(jnp.int32, shape, 1)
    rows = lax.broadcasted_iota(jnp.int32, shape, 0)
    own_head = lax.rem(columns, kv_heads) == rows // per_kv
    places = jnp.where(own_head, columns // kv_heads, span)

    stores = []
    visible = []
    for slot in range(slots):
        length = lengths_ref[me, slot]
        length = jnp.where(first == slot, lengths_ref[other, migrant_ref[other, 0]], length)
        length = jnp.where(second == slot, lengths_ref[other, migrant_ref[other, 1]], length)
        visible.append(length)
        held[slot, pl.ds(length, 1)] = fresh_ref[0, pl.ds(slot, 1)]
        copy = pltpu.make_async_copy(held.at[slot], out_ref.at[0, slot], store_sems.at[slot])
        copy.start()
        stores.append(copy)

    for slot in range(slots):
        keys = held[slot, :, :, :head_dim].reshape(span * kv_heads, head_dim)
        values = held[slot, :, :, head_dim:].reshape(span * kv_heads, head_dim)
        scores = lax.dot_general(
            query_ref[0, slot],
            keys,
            (((1,), (1,)), ((), ())),
            preferred_element_type=jnp.float32,
        ) * (1.0 / math.sqrt(head_dim))
        scores = jnp.where(places <= visible[slot], scores, -1e30)
        weights = jnp.exp(scores - jnp.max(scores, axis=-1, keepdims=True))
        probs = weights / jnp.sum(weights, axis=-1, keepdims=True)
        attended_ref[0, slot] = jnp.dot(
            probs.astype(jnp.bfloat16), values, preferred_element_type=jnp.float32
        ).astype(jnp.bfloat16)

    for copy in stores:
        copy.wait()


def local(
    cache,
    lengths,
    partner,
    migrant,
    replica_prefill_pages,
    page_dest,
    landing,
    query,
    fresh_key_value,
):
    replicas = lax.axis_size("replica")
    me = lax.axis_index("replica")
    _, slots, span, kv_heads, width = cache.shape
    page_len = replica_prefill_pages.shape[2]
    smem = pl.BlockSpec(memory_space=pltpu.SMEM)
    vmem = pl.BlockSpec(memory_space=pltpu.VMEM)
    hbm = pl.BlockSpec(memory_space=pl.ANY)

    pages = lax.all_gather(replica_prefill_pages[0], "replica", axis=0, tiled=True)
    outgoing = pl.pallas_call(
        pick_kernel,
        out_shape=jax.ShapeDtypeStruct((2, span, kv_heads, width), cache.dtype),
        in_specs=[smem, hbm],
        out_specs=hbm,
        scratch_shapes=[pltpu.SemaphoreType.DMA((2,))],
    )(migrant, cache)

    flipped = jnp.bitwise_xor(partner[me], me)
    bits = replicas.bit_length() - 1
    bit = jnp.sum((flipped >= 2 ** jnp.arange(1, bits)).astype(jnp.int32))

    def swap(distance, value):
        pairs = [(source, source ^ (1 << distance)) for source in range(replicas)]
        return lax.ppermute(value, "replica", pairs)

    arrived = lax.switch(bit, [functools.partial(swap, b) for b in range(bits)], outgoing)

    return pl.pallas_call(
        finish_kernel,
        out_shape=(
            jax.ShapeDtypeStruct(cache.shape, cache.dtype),
            jax.ShapeDtypeStruct(query.shape, query.dtype),
        ),
        in_specs=[smem] * 5 + [hbm] * 3 + [vmem] * 2,
        out_specs=(hbm, vmem),
        scratch_shapes=[
            pltpu.VMEM((slots, span, kv_heads, width), cache.dtype),
            pltpu.SemaphoreType.DMA((slots,)),
            pltpu.SemaphoreType.DMA((replicas * CAP,)),
            pltpu.SemaphoreType.DMA((slots,)),
        ],
        compiler_params=pltpu.CompilerParams(vmem_limit_bytes=40 * 1024 * 1024),
    )(
        lengths,
        partner,
        migrant,
        page_dest.reshape(-1),
        landing,
        cache,
        arrived,
        pages,
        query,
        fresh_key_value,
    )


def solution(mesh):
    cut = ("group", "replica")
    placed = (
        P(cut, None, None, "tensor", None),
        P("group", None),
        P("group"),
        P("group", None),
        P(cut, None, None, "tensor", None),
        P("group", None, None),
        P(cut, None),
        P(cut, None, "tensor", None),
        P(cut, None, "tensor", None),
    )
    return jax.shard_map(
        local,
        mesh=mesh,
        in_specs=placed,
        out_specs=(P(cut, None, None, "tensor", None), P(cut, None, "tensor", None)),
        check_vma=False,
    )
```

```python
import functools
import math

import jax
import jax.numpy as jnp
from jax import lax
from jax.experimental import pallas as pl
from jax.experimental.pallas import tpu as pltpu
from jax.sharding import PartitionSpec as P

CAP = 2


def pick_kernel(
    partner_ref, migrant_ref, dest_ref, cache_ref, pages_ref, out_ref, outbox_ref, bit_ref, sems
):
    me = lax.axis_index("replica")
    replicas = outbox_ref.shape[0]
    copies = [
        pltpu.make_async_copy(cache_ref.at[0, migrant_ref[m, me]], out_ref.at[m], sems.at[m])
        for m in range(2)
    ]
    for copy in copies:
        copy.start()
    dests = [dest_ref[k, 0, me] for k in range(pages_ref.shape[1])]
    for k, dest in enumerate(dests):
        rank = jnp.int32(0)
        for earlier in dests[:k]:
            rank = rank + (earlier == dest).astype(jnp.int32)
        copy = pltpu.make_async_copy(
            pages_ref.at[0, k], outbox_ref.at[dest, rank], sems.at[2 + k]
        )
        copy.start()
        copies.append(copy)
    flipped = jnp.bitwise_xor(partner_ref[me], me)
    bit = jnp.int32(0)
    for b in range(1, replicas.bit_length() - 1):
        bit = bit + (flipped >= (1 << b)).astype(jnp.int32)
    bit_ref[0] = bit
    for copy in copies:
        copy.wait()


def finish_kernel(
    lengths_ref,
    partner_ref,
    migrant_ref,
    dest_ref,
    landing_ref,
    cache_ref,
    arrived_ref,
    pages_ref,
    query_ref,
    fresh_ref,
    out_ref,
    attended_ref,
    held,
    load_sems,
    page_sems,
    store_sems,
):
    me = lax.axis_index("replica")
    slots, span, kv_heads, width = held.shape
    head_dim = width // 2
    heads = query_ref.shape[2]
    per_kv = heads // kv_heads
    sources, cap, page_len = pages_ref.shape[:3]
    held_pages = dest_ref.shape[0]
    per_slot = span // page_len
    first, second = migrant_ref[0, me], migrant_ref[1, me]
    other = partner_ref[me]

    def load(slot, source):
        return pltpu.make_async_copy(source, held.at[slot], load_sems.at[slot])

    for slot in range(slots):
        staying = jnp.logical_and(first != slot, second != slot)

        @pl.when(staying)
        def _():
            load(slot, cache_ref.at[0, slot]).start()

    load(first, arrived_ref.at[0]).start()
    load(second, arrived_ref.at[1]).start()
    for slot in range(slots):
        load(slot, cache_ref.at[0, slot]).wait()

    def page_copy(source, turn, rank):
        place = landing_ref[0, rank]
        slot = place // per_slot
        start = (place - slot * per_slot) * page_len
        return pltpu.make_async_copy(
            pages_ref.at[source, turn], held.at[slot, pl.ds(start, page_len)], page_sems.at[rank]
        )

    def take_source(source, rank):
        turn = jnp.int32(0)
        for k in range(held_pages):
            mine = dest_ref[k, 0, source] == me

            @pl.when(mine)
            def _():
                page_copy(source, turn, rank).start()

            turn = turn + mine.astype(jnp.int32)
            rank = rank + mine.astype(jnp.int32)
        return rank

    arrivals = lax.fori_loop(0, sources, take_source, jnp.int32(0))

    def wait_page(rank, carry):
        page_copy(0, 0, rank).wait()
        return carry

    lax.fori_loop(0, arrivals, wait_page, 0)

    shape = (heads, span * kv_heads)
    columns = lax.broadcasted_iota(jnp.int32, shape, 1)
    rows = lax.broadcasted_iota(jnp.int32, shape, 0)
    own_head = lax.rem(columns, kv_heads) == rows // per_kv
    places = jnp.where(own_head, columns // kv_heads, span)

    stores = []
    visible = []
    for slot in range(slots):
        length = lengths_ref[me, slot]
        length = jnp.where(first == slot, lengths_ref[other, migrant_ref[0, other]], length)
        length = jnp.where(second == slot, lengths_ref[other, migrant_ref[1, other]], length)
        visible.append(length)
        held[slot, pl.ds(length, 1)] = fresh_ref[0, pl.ds(slot, 1)]
        copy = pltpu.make_async_copy(held.at[slot], out_ref.at[0, slot], store_sems.at[slot])
        copy.start()
        stores.append(copy)

    for slot in range(slots):
        keys = held[slot, :, :, :head_dim].reshape(span * kv_heads, head_dim)
        values = held[slot, :, :, head_dim:].reshape(span * kv_heads, head_dim)
        scores = lax.dot_general(
            query_ref[0, slot],
            keys,
            (((1,), (1,)), ((), ())),
            preferred_element_type=jnp.float32,
        ) * (1.0 / math.sqrt(head_dim))
        scores = jnp.where(places <= visible[slot], scores, -1e30)
        weights = jnp.exp(scores - jnp.max(scores, axis=-1, keepdims=True))
        probs = weights / jnp.sum(weights, axis=-1, keepdims=True)
        attended_ref[0, slot] = jnp.dot(
            probs.astype(jnp.bfloat16), values, preferred_element_type=jnp.float32
        ).astype(jnp.bfloat16)

    for copy in stores:
        copy.wait()


def local(
    cache,
    lengths,
    partner,
    migrant,
    replica_prefill_pages,
    page_dest,
    landing,
    query,
    fresh_key_value,
):
    replicas = lax.axis_size("replica")
    _, slots, span, kv_heads, width = cache.shape
    page_len = replica_prefill_pages.shape[2]
    smem = pl.BlockSpec(memory_space=pltpu.SMEM)
    vmem = pl.BlockSpec(memory_space=pltpu.VMEM)
    hbm = pl.BlockSpec(memory_space=pl.ANY)

    held_pages = replica_prefill_pages.shape[1]
    movers = jnp.swapaxes(migrant, 0, 1)
    dests = jnp.transpose(page_dest, (1, 2, 0))
    outgoing, outbox, bit = pl.pallas_call(
        pick_kernel,
        out_shape=(
            jax.ShapeDtypeStruct((2, span, kv_heads, width), cache.dtype),
            jax.ShapeDtypeStruct((replicas, CAP, page_len, kv_heads, width), cache.dtype),
            jax.ShapeDtypeStruct((1,), jnp.int32),
        ),
        in_specs=[smem, smem, smem, hbm, hbm],
        out_specs=(hbm, hbm, smem),
        scratch_shapes=[pltpu.SemaphoreType.DMA((2 + held_pages,))],
    )(partner, movers, dests, cache, replica_prefill_pages)
    pages = lax.all_to_all(outbox, "replica", split_axis=0, concat_axis=0, tiled=True)
    bits = replicas.bit_length() - 1

    def swap(distance, value):
        pairs = [(source, source ^ (1 << distance)) for source in range(replicas)]
        return lax.ppermute(value, "replica", pairs)

    arrived = lax.switch(bit[0], [functools.partial(swap, b) for b in range(bits)], outgoing)

    return pl.pallas_call(
        finish_kernel,
        out_shape=(
            jax.ShapeDtypeStruct(cache.shape, cache.dtype),
            jax.ShapeDtypeStruct(query.shape, query.dtype),
        ),
        in_specs=[smem] * 5 + [hbm] * 3 + [vmem] * 2,
        out_specs=(hbm, vmem),
        scratch_shapes=[
            pltpu.VMEM((slots, span, kv_heads, width), cache.dtype),
            pltpu.SemaphoreType.DMA((slots,)),
            pltpu.SemaphoreType.DMA((replicas * CAP,)),
            pltpu.SemaphoreType.DMA((slots,)),
        ],
        compiler_params=pltpu.CompilerParams(vmem_limit_bytes=60 * 1024 * 1024),
    )(
        lengths,
        partner,
        movers,
        dests,
        landing,
        cache,
        arrived,
        pages,
        query,
        fresh_key_value,
    )


def solution(mesh):
    cut = ("group", "replica")
    placed = (
        P(cut, None, None, "tensor", None),
        P("group", None),
        P("group"),
        P("group", None),
        P(cut, None, None, "tensor", None),
        P("group", None, None),
        P(cut, None),
        P(cut, None, "tensor", None),
        P(cut, None, "tensor", None),
    )
    return jax.shard_map(
        local,
        mesh=mesh,
        in_specs=placed,
        out_specs=(P(cut, None, None, "tensor", None), P(cut, None, "tensor", None)),
        check_vma=False,
    )
```

```python
import functools
import math

import jax
import jax.numpy as jnp
from jax import lax
from jax.experimental import pallas as pl
from jax.experimental.pallas import tpu as pltpu
from jax.sharding import PartitionSpec as P

CAP = 2


def fetch(sources, targets, sems):
    copies = [
        pltpu.make_async_copy(source, target, sems.at[i])
        for i, (source, target) in enumerate(zip(sources, targets))
    ]
    for copy in copies:
        copy.start()
    return copies


def pick_kernel(
    partner_hbm,
    migrant_hbm,
    dest_hbm,
    cache_ref,
    pages_ref,
    out_ref,
    outbox_ref,
    bit_ref,
    partner_ref,
    migrant_ref,
    dest_ref,
    index_sems,
    sems,
):
    indices = fetch(
        (partner_hbm, migrant_hbm, dest_hbm), (partner_ref, migrant_ref, dest_ref), index_sems
    )
    for copy in indices:
        copy.wait()
    me = lax.axis_index("replica")
    replicas = outbox_ref.shape[0]
    copies = [
        pltpu.make_async_copy(cache_ref.at[0, migrant_ref[m, me]], out_ref.at[m], sems.at[m])
        for m in range(2)
    ]
    for copy in copies:
        copy.start()
    dests = [dest_ref[k, 0, me] for k in range(pages_ref.shape[1])]
    for k, dest in enumerate(dests):
        rank = jnp.int32(0)
        for earlier in dests[:k]:
            rank = rank + (earlier == dest).astype(jnp.int32)
        copy = pltpu.make_async_copy(
            pages_ref.at[0, k], outbox_ref.at[dest, rank], sems.at[2 + k]
        )
        copy.start()
        copies.append(copy)
    flipped = jnp.bitwise_xor(partner_ref[me], me)
    bit = jnp.int32(0)
    for b in range(1, replicas.bit_length() - 1):
        bit = bit + (flipped >= (1 << b)).astype(jnp.int32)
    bit_ref[0] = bit
    for copy in copies:
        copy.wait()


def finish_kernel(
    lengths_hbm,
    partner_hbm,
    migrant_hbm,
    dest_hbm,
    landing_hbm,
    cache_ref,
    arrived_ref,
    pages_ref,
    query_ref,
    fresh_ref,
    out_ref,
    attended_ref,
    lengths_ref,
    partner_ref,
    migrant_ref,
    dest_ref,
    landing_ref,
    index_sems,
    held,
    load_sems,
    page_sems,
    store_sems,
):
    me = lax.axis_index("replica")
    slots, span, kv_heads, width = held.shape
    head_dim = width // 2
    heads = query_ref.shape[2]
    per_kv = heads // kv_heads
    sources, cap, page_len = pages_ref.shape[:3]
    held_pages = dest_ref.shape[0]
    per_slot = span // page_len
    indices = fetch(
        (lengths_hbm, partner_hbm, migrant_hbm, dest_hbm, landing_hbm),
        (lengths_ref, partner_ref, migrant_ref, dest_ref, landing_ref),
        index_sems,
    )
    for copy in indices:
        copy.wait()
    first, second = migrant_ref[0, me], migrant_ref[1, me]
    other = partner_ref[me]

    def load(slot, source):
        return pltpu.make_async_copy(source, held.at[slot], load_sems.at[slot])

    for slot in range(slots):
        staying = jnp.logical_and(first != slot, second != slot)

        @pl.when(staying)
        def _():
            load(slot, cache_ref.at[0, slot]).start()

    load(first, arrived_ref.at[0]).start()
    load(second, arrived_ref.at[1]).start()
    for slot in range(slots):
        load(slot, cache_ref.at[0, slot]).wait()

    def page_copy(source, turn, rank):
        place = landing_ref[0, rank]
        slot = place // per_slot
        start = (place - slot * per_slot) * page_len
        return pltpu.make_async_copy(
            pages_ref.at[source, turn], held.at[slot, pl.ds(start, page_len)], page_sems.at[rank]
        )

    def take_source(source, rank):
        turn = jnp.int32(0)
        for k in range(held_pages):
            mine = dest_ref[k, 0, source] == me

            @pl.when(mine)
            def _():
                page_copy(source, turn, rank).start()

            turn = turn + mine.astype(jnp.int32)
            rank = rank + mine.astype(jnp.int32)
        return rank

    arrivals = lax.fori_loop(0, sources, take_source, jnp.int32(0))

    def wait_page(rank, carry):
        page_copy(0, 0, rank).wait()
        return carry

    lax.fori_loop(0, arrivals, wait_page, 0)

    shape = (heads, span * kv_heads)
    columns = lax.broadcasted_iota(jnp.int32, shape, 1)
    rows = lax.broadcasted_iota(jnp.int32, shape, 0)
    own_head = lax.rem(columns, kv_heads) == rows // per_kv
    places = jnp.where(own_head, columns // kv_heads, span)

    stores = []
    visible = []
    for slot in range(slots):
        length = lengths_ref[me, slot]
        length = jnp.where(first == slot, lengths_ref[other, migrant_ref[0, other]], length)
        length = jnp.where(second == slot, lengths_ref[other, migrant_ref[1, other]], length)
        visible.append(length)
        held[slot, pl.ds(length, 1)] = fresh_ref[0, pl.ds(slot, 1)]
        copy = pltpu.make_async_copy(held.at[slot], out_ref.at[0, slot], store_sems.at[slot])
        copy.start()
        stores.append(copy)

    for slot in range(slots):
        keys = held[slot, :, :, :head_dim].reshape(span * kv_heads, head_dim)
        values = held[slot, :, :, head_dim:].reshape(span * kv_heads, head_dim)
        scores = lax.dot_general(
            query_ref[0, slot],
            keys,
            (((1,), (1,)), ((), ())),
            preferred_element_type=jnp.float32,
        ) * (1.0 / math.sqrt(head_dim))
        scores = jnp.where(places <= visible[slot], scores, -1e30)
        weights = jnp.exp(scores - jnp.max(scores, axis=-1, keepdims=True))
        probs = weights / jnp.sum(weights, axis=-1, keepdims=True)
        attended_ref[0, slot] = jnp.dot(
            probs.astype(jnp.bfloat16), values, preferred_element_type=jnp.float32
        ).astype(jnp.bfloat16)

    for copy in stores:
        copy.wait()


def local(
    cache,
    lengths,
    partner,
    migrant,
    replica_prefill_pages,
    page_dest,
    landing,
    query,
    fresh_key_value,
):
    replicas = lax.axis_size("replica")
    _, slots, span, kv_heads, width = cache.shape
    page_len = replica_prefill_pages.shape[2]
    smem = pl.BlockSpec(memory_space=pltpu.SMEM)
    vmem = pl.BlockSpec(memory_space=pltpu.VMEM)
    hbm = pl.BlockSpec(memory_space=pl.ANY)
    fixed = pl.BlockSpec(memory_space=pltpu.HBM)

    held_pages = replica_prefill_pages.shape[1]
    movers = jnp.swapaxes(migrant, 0, 1)
    dests = jnp.transpose(page_dest, (1, 2, 0))
    outgoing, outbox, bit = pl.pallas_call(
        pick_kernel,
        out_shape=(
            jax.ShapeDtypeStruct((2, span, kv_heads, width), cache.dtype),
            jax.ShapeDtypeStruct((replicas, CAP, page_len, kv_heads, width), cache.dtype),
            jax.ShapeDtypeStruct((1,), jnp.int32),
        ),
        in_specs=[hbm] * 3 + [fixed, hbm],
        out_specs=(hbm, vmem, smem),
        scratch_shapes=[pltpu.SMEM(index.shape, index.dtype) for index in (partner, movers, dests)]
        + [pltpu.SemaphoreType.DMA((3,)), pltpu.SemaphoreType.DMA((2 + held_pages,))],
    )(partner, movers, dests, cache, replica_prefill_pages)
    pages = lax.all_to_all(outbox, "replica", split_axis=0, concat_axis=0, tiled=True)
    bits = replicas.bit_length() - 1

    def swap(distance, value):
        pairs = [(source, source ^ (1 << distance)) for source in range(replicas)]
        return lax.ppermute(value, "replica", pairs)

    arrived = lax.switch(bit[0], [functools.partial(swap, b) for b in range(bits)], outgoing)

    return pl.pallas_call(
        finish_kernel,
        out_shape=(
            jax.ShapeDtypeStruct(cache.shape, cache.dtype),
            jax.ShapeDtypeStruct(query.shape, query.dtype),
        ),
        in_specs=[hbm] * 5 + [fixed] + [hbm] * 2 + [vmem] * 2,
        out_specs=(hbm, vmem),
        scratch_shapes=[
            pltpu.SMEM(index.shape, index.dtype)
            for index in (lengths, partner, movers, dests, landing)
        ]
        + [
            pltpu.SemaphoreType.DMA((5,)),
            pltpu.VMEM((slots, span, kv_heads, width), cache.dtype),
            pltpu.SemaphoreType.DMA((slots,)),
            pltpu.SemaphoreType.DMA((replicas * CAP,)),
            pltpu.SemaphoreType.DMA((slots,)),
        ],
        compiler_params=pltpu.CompilerParams(vmem_limit_bytes=58 * 1024 * 1024),
    )(
        lengths,
        partner,
        movers,
        dests,
        landing,
        cache,
        arrived,
        pages,
        query,
        fresh_key_value,
    )


def solution(mesh):
    cut = ("group", "replica")
    placed = (
        P(cut, None, None, "tensor", None),
        P("group", None),
        P("group"),
        P("group", None),
        P(cut, None, None, "tensor", None),
        P("group", None, None),
        P(cut, None),
        P(cut, None, "tensor", None),
        P(cut, None, "tensor", None),
    )
    return jax.shard_map(
        local,
        mesh=mesh,
        in_specs=placed,
        out_specs=(P(cut, None, None, "tensor", None), P(cut, None, "tensor", None)),
        check_vma=False,
    )
```
